32 devices in a mesh: rep: 4 (over x, core), exp: 8 (over z, y).
Axes of the slice: x: 2, y: 2, z: 4, core: 2. Of those that a mesh axis runs over, the one named last changes fastest.
Arguments:
- trainer_weight: bfloat16 [64, 128, 7168], P('exp', None, 'rep'), may hold values from -0.125 to 0.125
- dirty: int32 [64], replicated, may hold values from 0 to 1, as said below
- rollout_owner: int32 [64], replicated, may hold values from 0 to 7, as said below
- rollout_slot: int32 [64], replicated, may hold values from 0 to 7, as said below
Outputs:
- update_tiles: bfloat16 [48, 128, 7168], P('exp')
- update_scales: bfloat16 [48, 1, 56], P('exp')
The draws below stay inside these ranges and needn't reach their ends.
Inputs may be any that keep to these rules, and one draw needn't show every extreme that they name: At most 6 dirty experts share a rollout owner, and exactly 6 do at one owner or more. `rollout_owner`: every rollout owner holds exactly 8 experts, and no two experts e, f with e // 8 == f // 8 share a rollout owner. `rollout_slot`: the 8 experts of one rollout owner have different slots.
All inputs are finite; a program needn't handle non-finite values.
Results may differ from the reference program's by a relative error of at most 0.0011.
Values may be sent and summed in bfloat16 or wider, within the bound.
No kernel may reach another device: no remote copies, remote signals or barrier semaphores. Data moves between devices by JAX's collectives and lax.ppermute only.
A program may use at most 128 MiB of HBM per device.

```python
import jax
import jax.numpy as jnp
from jax import lax

D = 7168
EXP_DEV = 8
SLAB = 128
B = 128
CAP = 6
E = 64
N_EXP = 8


def layout(key):
    keys = jax.random.split(key, 6)
    owners = E // EXP_DEV
    shuffle = jax.random.permutation(keys[0], owners).astype(jnp.int32)
    offsets = jax.random.permutation(keys[1], owners)[:EXP_DEV].astype(jnp.int32)
    expert = jnp.arange(E, dtype=jnp.int32)
    trainer = expert // EXP_DEV
    local = expert % EXP_DEV
    owner = ((shuffle[trainer] + offsets[local]) % owners).astype(jnp.int32)
    scores = jax.random.permutation(keys[2], E).astype(jnp.int32).reshape(owners, EXP_DEV)
    order = jnp.argsort(scores, axis=1).astype(jnp.int32)
    slot = order[owner, local].astype(jnp.int32)
    load = jax.random.randint(keys[3], (owners,), CAP - 2, CAP + 1).astype(jnp.int32)
    heavy = jax.random.randint(keys[4], (), 0, owners)
    load = jnp.where(jnp.arange(owners) == heavy, CAP, load).astype(jnp.int32)
    second = jax.random.permutation(keys[5], E).astype(jnp.int32).reshape(owners, EXP_DEV)
    picked = jnp.argsort(second, axis=1).astype(jnp.int32)
    dirty = (picked[owner, slot] < load[owner]).astype(jnp.int32)
    return (dirty, owner, slot)


def draw_dirty(key, part):
    shared = layout(key)
    return shared[0]


def draw_rollout_owner(key, part):
    shared = layout(key)
    return shared[1]


def draw_rollout_slot(key, part):
    shared = layout(key)
    return shared[2]


def level_of(rng, extent, cuts, least, high):
    def one(axis_at, blocks):
        steps = jax.random.uniform(jax.random.fold_in(jax.random.fold_in(rng, 6), axis_at), (blocks,), jnp.float32, least / len(cuts), high / len(cuts))
        return jnp.repeat(jnp.exp(steps), extent[axis_at] // blocks).reshape((-1,) + (1,) * (len(extent) - axis_at - 1))

    loudness = one(*cuts[0])
    for cut in cuts[1:]:
        loudness = loudness * one(*cut)
    return loudness


def gaussian(stream_key, extent, scale, bound, pieces=(), kind=jnp.bfloat16):
    values = scale * jax.random.normal(stream_key, extent, jnp.float32)
    if pieces:
        values = values * level_of(stream_key, extent, pieces, -0.22, 0.18)
    return jnp.clip(values, -bound, bound).astype(kind)


def setup_inputs(seed: int = 0) -> dict:
    key_list = jax.random.split(jax.random.key(seed), 5)
    return {
        "trainer_weight": gaussian(key_list[0], (E, SLAB, D), 2048 ** -0.5, 0.125, ((0, 8), (2, 4))),
        "dirty": draw_dirty(jax.random.fold_in(key_list[4], 71), 0),
        "rollout_owner": draw_rollout_owner(jax.random.fold_in(key_list[4], 71), 0),
        "rollout_slot": draw_rollout_slot(jax.random.fold_in(key_list[4], 71), 0),
    }


def reference(trainer_weight, dirty, rollout_owner, rollout_slot):
    blocks = trainer_weight.astype(jnp.float32).reshape(E, SLAB // B, B, D // B, B)
    largest = jnp.max(jnp.abs(blocks), axis=(2, 4))
    scale = (largest + 1e-6).astype(jnp.bfloat16)
    divisor = lax.optimization_barrier(scale).astype(jnp.float32)
    scaled = (blocks / divisor[:, :, None, :, None]).reshape(E, SLAB, D).astype(jnp.bfloat16)
    live = dirty == 1
    earlier = (rollout_owner[:, None] == rollout_owner[None, :]) & live[None, :] & (rollout_slot[None, :] < rollout_slot[:, None])
    rank = jnp.sum(earlier.astype(jnp.int32), axis=1).astype(jnp.int32)
    target = jnp.where(live, rollout_owner * CAP + rank, N_EXP * CAP).astype(jnp.int32)
    update_tiles = jnp.zeros((N_EXP * CAP, SLAB, D), jnp.bfloat16).at[target].set(scaled, mode="drop")
    update_scales = jnp.zeros((N_EXP * CAP, SLAB // B, D // B), jnp.bfloat16).at[target].set(scale, mode="drop")
    return update_tiles, update_scales
```

```python
import functools

import jax
import jax.numpy as jnp
from jax import lax
from jax.experimental import pallas as pl
from jax.experimental.pallas import tpu as pltpu
from jax.sharding import PartitionSpec as P

B = 128
CAP = 6

ORDER = (0, 1, 2, 3, 4, 5, 6, 7)
LIMIT = (3, 4, 5, 6, 7, 8)
GROUPS = ((0, 1, 2), (3, 4), (5,))
PICK, ROW, LIVE = 0, 8, 16
VMEM_LIMIT = 8 * 1024 * 1024
PLACE_LIMIT = 24 * 1024 * 1024

ANY = pl.BlockSpec(memory_space=pl.ANY)
HBM = pl.BlockSpec(memory_space=pltpu.HBM)
VMEM = pl.BlockSpec(memory_space=pltpu.VMEM)
SMEM = pl.BlockSpec(memory_space=pltpu.SMEM)


def expert_for(owner_ref, source, dest, local_count):
    found = jnp.int32(0)
    for j in range(local_count):
        at = source * local_count + j
        found = jnp.where(owner_ref[at] == dest, at, found)
    return found


def pick_kernel(shifts, local_count, owner_ref, w_ref, *refs):
    outs, sems = refs[:-1], refs[-1]
    here = lax.axis_index("exp")
    copies = []
    for i, shift in enumerate(shifts):
        local = expert_for(owner_ref, here, here ^ shift, local_count) - here * local_count
        copies.append(pltpu.make_async_copy(w_ref.at[local], outs[i], sems.at[i]))
        copies[-1].start()
    for copy in copies:
        copy.wait()


def pick(owner, weight, shifts):
    local_count, rows, cols = weight.shape
    return pl.pallas_call(
        functools.partial(pick_kernel, shifts, local_count),
        out_shape=[jax.ShapeDtypeStruct((rows, cols), weight.dtype)] * len(shifts),
        in_specs=[SMEM, HBM],
        out_specs=[VMEM] * len(shifts),
        scratch_shapes=[pltpu.SemaphoreType.DMA((len(shifts),))],
        compiler_params=pltpu.CompilerParams(vmem_limit_bytes=VMEM_LIMIT),
        name="pick",
    )(owner, weight)


def table_kernel(local_count, owner_ref, dirty_ref, slot_ref, out_ref):
    here = lax.axis_index("exp")
    live, slot = [], []
    for shift in ORDER:
        expert = expert_for(owner_ref, here ^ shift, here, local_count)
        live.append((dirty_ref[expert] == 1).astype(jnp.int32))
        slot.append(slot_ref[expert])
    rank = [
        sum(live[k] * (slot[k] < slot[m]).astype(jnp.int32) for k in range(len(ORDER)) if k != m)
        for m in range(len(ORDER))
    ]
    spare, left = sum(live), list(live)
    for j, limit in enumerate(LIMIT):
        found, pick, row = jnp.int32(0), jnp.int32(0), spare
        for m in range(limit):
            take = left[m] * (1 - found)
            pick = jnp.where(take == 1, m, pick)
            row = jnp.where(take == 1, rank[m], row)
            left[m] = left[m] - take
            found = found + take
        spare = spare + 1 - found
        out_ref[PICK + j] = pick
        out_ref[ROW + j] = row
        out_ref[LIVE + j] = found


def routing_table(owner, dirty, slot, local_count):
    return pl.pallas_call(
        functools.partial(table_kernel, local_count),
        out_shape=jax.ShapeDtypeStruct((24,), jnp.int32),
        in_specs=[SMEM] * 3,
        out_specs=SMEM,
        compiler_params=pltpu.CompilerParams(vmem_limit_bytes=VMEM_LIMIT),
        name="routing_table",
    )(owner, dirty, slot)


def pack_kernel(j, count, table_ref, *refs):
    out_ref, sem = refs[-2:]
    for m in range(count):

        @pl.when(table_ref[PICK + j] == m)
        def _():
            pltpu.make_async_copy(refs[m], out_ref, sem).start()

    pltpu.make_async_copy(out_ref, out_ref, sem).wait()


def pack(table, arrived, j, tokens):
    return pl.pallas_call(
        functools.partial(pack_kernel, j, len(arrived)),
        out_shape=jax.ShapeDtypeStruct(arrived[0].shape, arrived[0].dtype),
        in_specs=[SMEM] + [ANY] * (len(arrived) + len(tokens)),
        out_specs=VMEM,
        scratch_shapes=[pltpu.SemaphoreType.DMA],
        compiler_params=pltpu.CompilerParams(vmem_limit_bytes=VMEM_LIMIT),
        name="pack",
    )(table, *arrived, *tokens)


def place_kernel(spots, fresh, table_ref, *refs):
    arrays, refs = refs[: len(spots)], refs[len(spots) :]
    if not fresh:
        acc_in, refs = refs[1], refs[2:]
    out_ref, acc_out, acc_ref, held, sems = refs
    rows, cols = arrays[0].shape
    here = lax.axis_index("rep")
    line = lax.broadcasted_iota(jnp.int32, acc_ref.shape, 0)
    lane = lax.broadcasted_iota(jnp.int32, acc_ref.shape, 1)
    acc_ref[...] = jnp.zeros_like(acc_ref) if fresh else acc_in[...]
    copies = []
    for i, (j, flip) in enumerate(spots):
        first = pl.multiple_of((here ^ flip) * cols, B)
        first_block = (here ^ flip) * (cols // B)
        row = table_ref[ROW + j]
        live = table_ref[LIVE + j] == 1
        at = i * cols

        @pl.when(live)
        def _():
            acc = acc_ref[...]
            for c in range(0, cols, B):
                x = arrays[i][:, c : c + B]
                most = jnp.max(jnp.abs(x), axis=0, keepdims=True).astype(jnp.float32)
                most = jnp.max(most, axis=1, keepdims=True)
                scale = (most + 1e-06).astype(jnp.bfloat16).astype(jnp.float32)
                scaled = x.astype(jnp.float32) * (1.0 / scale)
                held[:, at + c : at + c + B] = scaled.astype(jnp.bfloat16)
                acc = jnp.where((line == row) & (lane == first_block + c // B), scale, acc)
            acc_ref[...] = acc

        @pl.when(jnp.logical_not(live))
        def _():
            held[:, at : at + cols] = jnp.zeros((rows, cols), jnp.bfloat16)

        copies.append(
            pltpu.make_async_copy(
                held.at[:, pl.ds(at, cols)], out_ref.at[row, :, pl.ds(first, cols)], sems.at[i]
            )
        )
        copies[-1].start()

    acc = acc_ref[...]
    acc_out[...] = acc[: acc_out.shape[0], : acc_out.shape[1]].astype(acc_out.dtype)
    for copy in copies:
        copy.wait()


def place(state, table, arrays, spots, replicas, final):
    rows, cols = arrays[0].shape
    fresh = state is None
    kept = jax.ShapeDtypeStruct((8, 128), jnp.float32)
    scales = jax.ShapeDtypeStruct((CAP, cols * replicas // B), jnp.bfloat16)
    return pl.pallas_call(
        functools.partial(place_kernel, spots, fresh),
        out_shape=[
            jax.ShapeDtypeStruct((CAP, rows, cols * replicas), jnp.bfloat16),
            scales if final else kept,
        ],
        in_specs=[SMEM] + [VMEM] * len(arrays) + ([] if fresh else [HBM, VMEM]),
        out_specs=[HBM, VMEM],
        scratch_shapes=[
            pltpu.VMEM(kept.shape, kept.dtype),
            pltpu.VMEM((rows, len(arrays) * cols), jnp.bfloat16),
            pltpu.SemaphoreType.DMA((len(arrays),)),
        ],
        input_output_aliases={} if fresh else {1 + len(arrays): 0},
        compiler_params=pltpu.CompilerParams(vmem_limit_bytes=PLACE_LIMIT),
        cost_estimate=pl.CostEstimate(
            flops=0, bytes_accessed=8 * rows * cols * len(arrays), transcendentals=0
        ),
        name="place",
    )(table, *arrays, *(state or ()))


def gate_kernel(x_ref, *refs):
    pass


def gate(x, *tokens):
    return pl.pallas_call(
        gate_kernel,
        out_shape=jax.ShapeDtypeStruct(x.shape, x.dtype),
        in_specs=[ANY] * (1 + len(tokens)),
        out_specs=ANY,
        input_output_aliases={0: 0},
        compiler_params=pltpu.CompilerParams(vmem_limit_bytes=VMEM_LIMIT),
        name="gate",
    )(x, *tokens)


def pairs(count, flip):
    return [(i, i ^ flip) for i in range(count)]


def paired(trainer_weight, dirty, rollout_owner, rollout_slot):
    replicas, owners = lax.axis_size("rep"), lax.axis_size("exp")
    local_count = trainer_weight.shape[0]

    def over_rep(x, flip):
        return lax.ppermute(x, "rep", pairs(replicas, flip))

    picked = (4, 1, 2, 3, 5, 0, 6, 7)
    outgoing = dict(zip(picked, pick(rollout_owner, trainer_weight, picked)))
    table = routing_table(rollout_owner, dirty, rollout_slot, local_count)
    after = {5: 1, 6: 3, 7: 4}
    got, packed, state = {}, [], None
    done = []
    for group in GROUPS:
        arrays, spots = [], []
        for j in group:
            for flip in ORDER[: LIMIT[j]]:
                if flip not in got:
                    x = outgoing[flip]
                    if flip in after:
                        x = gate(x, got[after[flip]])
                    got[flip] = lax.ppermute(x, "exp", pairs(owners, flip)) if flip else x
            final = j == CAP - 1
            mine = pack(table, [got[f] for f in ORDER[: LIMIT[j]]], j, [packed[-1], done[0]] if final else [])
            packed.append(mine)
            beside = over_rep(mine, 1)
            across = over_rep(mine, 2)
            diagonal = over_rep(gate(across, done[-1]) if final else across, 1)
            arrays += [mine, beside, across, diagonal]
            spots += [(j, flip) for flip in range(4)]
        state = place(state, table, arrays, tuple(spots), replicas, group == GROUPS[-1])
        done.append(state[1])
    tiles, scales = state
    return tiles, scales[:, None, :]


def quantize(weights):
    count, rows, cols = weights.shape
    blocks = weights.astype(jnp.float32).reshape(count, rows // B, B, cols // B, B)
    largest = jnp.max(jnp.abs(blocks), axis=(2, 4))
    scale = (largest + 1e-06).astype(jnp.bfloat16)
    divisor = lax.optimization_barrier(scale).astype(jnp.float32)
    scaled = (blocks / divisor[:, :, None, :, None]).reshape(count, rows, cols).astype(jnp.bfloat16)
    return (scaled, scale)


def gathered(trainer_weight, dirty, rollout_owner, rollout_slot):
    owners = lax.axis_size("exp")
    here = lax.axis_index("exp")
    local_count = trainer_weight.shape[0]
    experts = dirty.shape[0]
    live = dirty == 1
    earlier = (
        (rollout_owner[:, None] == rollout_owner[None, :])
        & live[None, :]
        & (rollout_slot[None, :] < rollout_slot[:, None])
    )
    rank = jnp.sum(earlier.astype(jnp.int32), axis=1)
    start = here * local_count
    local_owner = lax.dynamic_slice_in_dim(rollout_owner, start, local_count)
    local_live = lax.dynamic_slice_in_dim(live, start, local_count)
    peers = jnp.arange(owners, dtype=jnp.int32)
    outgoing = ((local_owner[None, :] == peers[:, None]) & local_live[None, :]).astype(jnp.bfloat16)
    slots = jnp.arange(CAP, dtype=jnp.int32)
    wanted = (
        live[None, :] & (rollout_owner[None, :] == here) & (rank[None, :] == slots[:, None])
    ).astype(jnp.float32)
    source = (
        jnp.arange(experts, dtype=jnp.int32)[:, None] // local_count == peers[None, :]
    ).astype(jnp.float32)
    pick = jnp.dot(
        wanted, source, precision=lax.Precision.HIGHEST, preferred_element_type=jnp.float32
    )
    pick_low = pick.astype(jnp.bfloat16)
    scaled, scale = quantize(trainer_weight)
    send_tiles = jnp.einsum(
        "pj,jsd->psd", outgoing, scaled, preferred_element_type=jnp.float32
    ).astype(jnp.bfloat16)
    send_scales = jnp.einsum(
        "pj,jab->pab", outgoing, scale, preferred_element_type=jnp.float32
    ).astype(jnp.bfloat16)
    got_tiles, got_scales = (
        lax.all_to_all(send_tiles, "exp", split_axis=0, concat_axis=0, tiled=True),
        lax.all_to_all(send_scales, "exp", split_axis=0, concat_axis=0, tiled=True),
    )
    tiles = jnp.einsum(
        "cp,psd->csd", pick_low, got_tiles, preferred_element_type=jnp.float32
    ).astype(jnp.bfloat16)
    scales = jnp.einsum(
        "cp,pab->cab", pick_low, got_scales, preferred_element_type=jnp.float32
    ).astype(jnp.bfloat16)
    update_tiles, update_scales = (
        lax.all_gather(tiles, "rep", axis=2, tiled=True),
        lax.all_gather(scales, "rep", axis=2, tiled=True),
    )
    return (update_tiles, update_scales)


def on_device(trainer_weight, dirty, rollout_owner, rollout_slot):
    local_count, rows, cols = trainer_weight.shape
    replicas, owners = lax.axis_size("rep"), lax.axis_size("exp")
    if (replicas, owners, local_count, rows) == (4, len(ORDER), len(ORDER), B) and cols % B == 0:
        return paired(trainer_weight, dirty, rollout_owner, rollout_slot)
    return gathered(trainer_weight, dirty, rollout_owner, rollout_slot)


def solution(mesh):
    in_specs = (P("exp", None, "rep"), P(), P(), P())
    out_specs = (P("exp", None, None), P("exp", None, None))
    return jax.shard_map(
        on_device, mesh=mesh, in_specs=in_specs, out_specs=out_specs, check_vma=False
    )
```

```python
import functools

import jax
import jax.numpy as jnp
from jax import lax
from jax.experimental import pallas as pl
from jax.experimental.pallas import tpu as pltpu
from jax.sharding import PartitionSpec as P

B = 128
CAP = 6

ORDER = (0, 1, 2, 3, 4, 5, 7, 6)
LIMIT = (3, 4, 5, 6, 7, 8)
ALL = (0, 1, 2, 3)
WAVES = (((0, ALL), (1, ALL), (2, ALL)), ((3, ALL), (4, ALL), (5, (0, 1))), ((5, (2, 3)),))
PICK, ROW, LIVE = 0, 8, 16
VMEM_LIMIT = 8 * 1024 * 1024
PLACE_LIMIT = 24 * 1024 * 1024

ANY = pl.BlockSpec(memory_space=pl.ANY)
HBM = pl.BlockSpec(memory_space=pltpu.HBM)
VMEM = pl.BlockSpec(memory_space=pltpu.VMEM)
SMEM = pl.BlockSpec(memory_space=pltpu.SMEM)


def expert_for(owner_ref, source, dest, local_count):
    found = jnp.int32(0)
    for j in range(local_count):
        at = source * local_count + j
        found = jnp.where(owner_ref[at] == dest, at, found)
    return found


def pick_kernel(shifts, local_count, owner_ref, w_ref, *refs):
    outs, sems = refs[:-1], refs[-1]
    here = lax.axis_index("exp")
    copies = []
    for i, shift in enumerate(shifts):
        local = expert_for(owner_ref, here, here ^ shift, local_count) - here * local_count
        copies.append(pltpu.make_async_copy(w_ref.at[local], outs[i], sems.at[i]))
        copies[-1].start()
    for copy in copies:
        copy.wait()


def pick(owner, weight, shifts):
    local_count, rows, cols = weight.shape
    return pl.pallas_call(
        functools.partial(pick_kernel, shifts, local_count),
        out_shape=[jax.ShapeDtypeStruct((rows, cols), weight.dtype)] * len(shifts),
        in_specs=[SMEM, HBM],
        out_specs=[VMEM] * len(shifts),
        scratch_shapes=[pltpu.SemaphoreType.DMA((len(shifts),))],
        compiler_params=pltpu.CompilerParams(vmem_limit_bytes=VMEM_LIMIT),
        name="pick",
    )(owner, weight)


def table_kernel(local_count, owner_ref, dirty_ref, slot_ref, out_ref):
    here = lax.axis_index("exp")
    live, slot = [], []
    for shift in ORDER:
        expert = expert_for(owner_ref, here ^ shift, here, local_count)
        live.append((dirty_ref[expert] == 1).astype(jnp.int32))
        slot.append(slot_ref[expert])
    rank = [
        sum(live[k] * (slot[k] < slot[m]).astype(jnp.int32) for k in range(len(ORDER)) if k != m)
        for m in range(len(ORDER))
    ]
    spare, left = sum(live), list(live)
    for j, limit in enumerate(LIMIT):
        found, pick, row = jnp.int32(0), jnp.int32(0), spare
        for m in range(limit):
            take = left[m] * (1 - found)
            pick = jnp.where(take == 1, m, pick)
            row = jnp.where(take == 1, rank[m], row)
            left[m] = left[m] - take
            found = found + take
        spare = spare + 1 - found
        out_ref[PICK + j] = pick
        out_ref[ROW + j] = row
        out_ref[LIVE + j] = found


def routing_table(owner, dirty, slot, local_count):
    return pl.pallas_call(
        functools.partial(table_kernel, local_count),
        out_shape=jax.ShapeDtypeStruct((24,), jnp.int32),
        in_specs=[SMEM] * 3,
        out_specs=SMEM,
        compiler_params=pltpu.CompilerParams(vmem_limit_bytes=VMEM_LIMIT),
        name="routing_table",
    )(owner, dirty, slot)


def pack_kernel(j, count, table_ref, *refs):
    out_ref, sem = refs[-2:]
    for m in range(count):

        @pl.when(table_ref[PICK + j] == m)
        def _():
            pltpu.make_async_copy(refs[m], out_ref, sem).start()

    pltpu.make_async_copy(out_ref, out_ref, sem).wait()


def pack(table, arrived, j, tokens):
    return pl.pallas_call(
        functools.partial(pack_kernel, j, len(arrived)),
        out_shape=jax.ShapeDtypeStruct(arrived[0].shape, arrived[0].dtype),
        in_specs=[SMEM] + [ANY] * (len(arrived) + len(tokens)),
        out_specs=VMEM,
        scratch_shapes=[pltpu.SemaphoreType.DMA],
        compiler_params=pltpu.CompilerParams(vmem_limit_bytes=VMEM_LIMIT),
        name="pack",
    )(table, *arrived, *tokens)


def place_kernel(spots, fresh, table_ref, *refs):
    arrays, refs = refs[: len(spots)], refs[len(spots) :]
    if not fresh:
        acc_in, refs = refs[1], refs[2:]
    out_ref, acc_out, acc_ref, held, sems = refs
    rows, cols = arrays[0].shape
    here = lax.axis_index("rep")
    line = lax.broadcasted_iota(jnp.int32, acc_ref.shape, 0)
    lane = lax.broadcasted_iota(jnp.int32, acc_ref.shape, 1)
    acc_ref[...] = jnp.zeros_like(acc_ref) if fresh else acc_in[...]
    copies = []
    for i, (j, flip) in enumerate(spots):
        first = pl.multiple_of((here ^ flip) * cols, B)
        first_block = (here ^ flip) * (cols // B)
        row = table_ref[ROW + j]
        live = table_ref[LIVE + j] == 1
        at = i * cols

        @pl.when(live)
        def _():
            acc = acc_ref[...]
            for c in range(0, cols, B):
                x = arrays[i][:, c : c + B]
                most = jnp.max(jnp.abs(x), axis=0, keepdims=True).astype(jnp.float32)
                most = jnp.max(most, axis=1, keepdims=True)
                scale = (most + 1e-06).astype(jnp.bfloat16).astype(jnp.float32)
                scaled = x.astype(jnp.float32) * (1.0 / scale)
                held[:, at + c : at + c + B] = scaled.astype(jnp.bfloat16)
                acc = jnp.where((line == row) & (lane == first_block + c // B), scale, acc)
            acc_ref[...] = acc

        @pl.when(jnp.logical_not(live))
        def _():
            held[:, at : at + cols] = jnp.zeros((rows, cols), jnp.bfloat16)

        copies.append(
            pltpu.make_async_copy(
                held.at[:, pl.ds(at, cols)], out_ref.at[row, :, pl.ds(first, cols)], sems.at[i]
            )
        )
        copies[-1].start()

    acc = acc_ref[...]
    acc_out[...] = acc[: acc_out.shape[0], : acc_out.shape[1]].astype(acc_out.dtype)
    for copy in copies:
        copy.wait()


def place(state, table, arrays, spots, replicas, final):
    rows, cols = arrays[0].shape
    fresh = state is None
    kept = jax.ShapeDtypeStruct((8, 128), jnp.float32)
    scales = jax.ShapeDtypeStruct((CAP, cols * replicas // B), jnp.bfloat16)
    return pl.pallas_call(
        functools.partial(place_kernel, spots, fresh),
        out_shape=[
            jax.ShapeDtypeStruct((CAP, rows, cols * replicas), jnp.bfloat16),
            scales if final else kept,
        ],
        in_specs=[SMEM] + [VMEM] * len(arrays) + ([] if fresh else [HBM, VMEM]),
        out_specs=[HBM, VMEM],
        scratch_shapes=[
            pltpu.VMEM(kept.shape, kept.dtype),
            pltpu.VMEM((rows, len(arrays) * cols), jnp.bfloat16),
            pltpu.SemaphoreType.DMA((len(arrays),)),
        ],
        input_output_aliases={} if fresh else {1 + len(arrays): 0},
        compiler_params=pltpu.CompilerParams(vmem_limit_bytes=PLACE_LIMIT),
        cost_estimate=pl.CostEstimate(
            flops=0, bytes_accessed=8 * rows * cols * len(arrays), transcendentals=0
        ),
        name="place",
    )(table, *arrays, *(state or ()))


def gate_kernel(x_ref, *refs):
    pass


def gate(x, *tokens):
    return pl.pallas_call(
        gate_kernel,
        out_shape=jax.ShapeDtypeStruct(x.shape, x.dtype),
        in_specs=[ANY] * (1 + len(tokens)),
        out_specs=ANY,
        input_output_aliases={0: 0},
        compiler_params=pltpu.CompilerParams(vmem_limit_bytes=VMEM_LIMIT),
        name="gate",
    )(x, *tokens)


def pairs(count, flip):
    return [(i, i ^ flip) for i in range(count)]


def paired(trainer_weight, dirty, rollout_owner, rollout_slot):
    replicas, owners = lax.axis_size("rep"), lax.axis_size("exp")
    local_count = trainer_weight.shape[0]

    def over_rep(x, flip):
        return lax.ppermute(x, "rep", pairs(replicas, flip))

    picked = (4, 1, 2, 3, 5, 0, 7, 6)
    outgoing = dict(zip(picked, pick(rollout_owner, trainer_weight, picked)))
    table = routing_table(rollout_owner, dirty, rollout_slot, local_count)
    after = {5: 1, 7: 3, 6: 4}
    got, held, state = {}, {}, None

    def arrival(flip):
        if flip not in got:
            x = outgoing[flip]
            if flip in after:
                x = gate(x, got[after[flip]])
            got[flip] = lax.ppermute(x, "exp", pairs(owners, flip)) if flip else x
        return got[flip]

    def shard(j, flip):
        if (j, flip) not in held:
            if flip == 0:
                tokens = [held[j - 1, 0], state[1]] if j == CAP - 1 else []
                held[j, 0] = pack(table, [arrival(f) for f in ORDER[: LIMIT[j]]], j, tokens)
            else:
                held[j, flip] = over_rep(held[j, 2 if flip == 3 else 0], 1 if flip & 1 else 2)
        return held[j, flip]

    for wave in WAVES:
        spots = tuple((j, flip) for j, flips in wave for flip in flips)
        arrays = [shard(j, flip) for j, flip in spots]
        state = place(state, table, arrays, spots, replicas, wave is WAVES[-1])
    tiles, scales = state
    return tiles, scales[:, None, :]


def quantize(weights):
    count, rows, cols = weights.shape
    blocks = weights.astype(jnp.float32).reshape(count, rows // B, B, cols // B, B)
    largest = jnp.max(jnp.abs(blocks), axis=(2, 4))
    scale = (largest + 1e-06).astype(jnp.bfloat16)
    divisor = lax.optimization_barrier(scale).astype(jnp.float32)
    scaled = (blocks / divisor[:, :, None, :, None]).reshape(count, rows, cols).astype(jnp.bfloat16)
    return (scaled, scale)


def gathered(trainer_weight, dirty, rollout_owner, rollout_slot):
    owners = lax.axis_size("exp")
    here = lax.axis_index("exp")
    local_count = trainer_weight.shape[0]
    experts = dirty.shape[0]
    live = dirty == 1
    earlier = (
        (rollout_owner[:, None] == rollout_owner[None, :])
        & live[None, :]
        & (rollout_slot[None, :] < rollout_slot[:, None])
    )
    rank = jnp.sum(earlier.astype(jnp.int32), axis=1)
    start = here * local_count
    local_owner = lax.dynamic_slice_in_dim(rollout_owner, start, local_count)
    local_live = lax.dynamic_slice_in_dim(live, start, local_count)
    peers = jnp.arange(owners, dtype=jnp.int32)
    outgoing = ((local_owner[None, :] == peers[:, None]) & local_live[None, :]).astype(jnp.bfloat16)
    slots = jnp.arange(CAP, dtype=jnp.int32)
    wanted = (
        live[None, :] & (rollout_owner[None, :] == here) & (rank[None, :] == slots[:, None])
    ).astype(jnp.float32)
    source = (
        jnp.arange(experts, dtype=jnp.int32)[:, None] // local_count == peers[None, :]
    ).astype(jnp.float32)
    pick = jnp.dot(
        wanted, source, precision=lax.Precision.HIGHEST, preferred_element_type=jnp.float32
    )
    pick_low = pick.astype(jnp.bfloat16)
    scaled, scale = quantize(trainer_weight)
    send_tiles = jnp.einsum(
        "pj,jsd->psd", outgoing, scaled, preferred_element_type=jnp.float32
    ).astype(jnp.bfloat16)
    send_scales = jnp.einsum(
        "pj,jab->pab", outgoing, scale, preferred_element_type=jnp.float32
    ).astype(jnp.bfloat16)
    got_tiles, got_scales = (
        lax.all_to_all(send_tiles, "exp", split_axis=0, concat_axis=0, tiled=True),
        lax.all_to_all(send_scales, "exp", split_axis=0, concat_axis=0, tiled=True),
    )
    tiles = jnp.einsum(
        "cp,psd->csd", pick_low, got_tiles, preferred_element_type=jnp.float32
    ).astype(jnp.bfloat16)
    scales = jnp.einsum(
        "cp,pab->cab", pick_low, got_scales, preferred_element_type=jnp.float32
    ).astype(jnp.bfloat16)
    update_tiles, update_scales = (
        lax.all_gather(tiles, "rep", axis=2, tiled=True),
        lax.all_gather(scales, "rep", axis=2, tiled=True),
    )
    return (update_tiles, update_scales)


def on_device(trainer_weight, dirty, rollout_owner, rollout_slot):
    local_count, rows, cols = trainer_weight.shape
    replicas, owners = lax.axis_size("rep"), lax.axis_size("exp")
    if (replicas, owners, local_count, rows) == (4, len(ORDER), len(ORDER), B) and cols % B == 0:
        return paired(trainer_weight, dirty, rollout_owner, rollout_slot)
    return gathered(trainer_weight, dirty, rollout_owner, rollout_slot)


def solution(mesh):
    in_specs = (P("exp", None, "rep"), P(), P(), P())
    out_specs = (P("exp", None, None), P("exp", None, None))
    return jax.shard_map(
        on_device, mesh=mesh, in_specs=in_specs, out_specs=out_specs, check_vma=False
    )
```

```python
import functools

import jax
import jax.numpy as jnp
from jax import lax
from jax.experimental import pallas as pl
from jax.experimental.pallas import tpu as pltpu
from jax.sharding import PartitionSpec as P

B = 128
CAP = 6

ORDER = (0, 1, 2, 3, 4, 5, 7, 6)
LIMIT = (3, 4, 5, 6, 7, 8)
ALL = (0, 1, 2, 3)
WAVES = (((0, ALL), (1, ALL), (2, ALL)), ((3, ALL), (4, ALL), (5, (0, 1))), ((5, (2, 3)),))
PICK, ROW, LIVE = 0, 8, 16
VMEM_LIMIT = 8 * 1024 * 1024
PLACE_LIMIT = 24 * 1024 * 1024
PICK_LIMIT = 48 * 1024 * 1024

ANY = pl.BlockSpec(memory_space=pl.ANY)
HBM = pl.BlockSpec(memory_space=pltpu.HBM)
VMEM = pl.BlockSpec(memory_space=pltpu.VMEM)
SMEM = pl.BlockSpec(memory_space=pltpu.SMEM)


def expert_for(owner_ref, source, dest, local_count):
    found = jnp.int32(0)
    for j in range(local_count):
        at = source * local_count + j
        found = jnp.where(owner_ref[at] == dest, at, found)
    return found


def pick_kernel(shifts, local_count, owner_ref, w_ref, *refs):
    outs, sems = refs[:-1], refs[-1]
    here = lax.axis_index("exp")
    copies = []
    for i, shift in enumerate(shifts):
        local = expert_for(owner_ref, here, here ^ shift, local_count) - here * local_count
        copies.append(pltpu.make_async_copy(w_ref.at[local], outs[i], sems.at[i]))
        copies[-1].start()
    for copy in copies:
        copy.wait()


def pick(owner, weight, shifts):
    local_count, rows, cols = weight.shape
    return pl.pallas_call(
        functools.partial(pick_kernel, shifts, local_count),
        out_shape=[jax.ShapeDtypeStruct((rows, cols), weight.dtype)] * len(shifts),
        in_specs=[SMEM, HBM],
        out_specs=[VMEM] * len(shifts),
        scratch_shapes=[pltpu.SemaphoreType.DMA((len(shifts),))],
        compiler_params=pltpu.CompilerParams(vmem_limit_bytes=PICK_LIMIT),
        name="pick",
    )(owner, weight)


def table_kernel(local_count, owner_ref, dirty_ref, slot_ref, out_ref):
    here = lax.axis_index("exp")
    live, slot = [], []
    for shift in ORDER:
        expert = expert_for(owner_ref, here ^ shift, here, local_count)
        live.append((dirty_ref[expert] == 1).astype(jnp.int32))
        slot.append(slot_ref[expert])
    rank = [
        sum(live[k] * (slot[k] < slot[m]).astype(jnp.int32) for k in range(len(ORDER)) if k != m)
        for m in range(len(ORDER))
    ]
    spare, left = sum(live), list(live)
    for j, limit in enumerate(LIMIT):
        found, pick, row = jnp.int32(0), jnp.int32(0), spare
        for m in range(limit):
            take = left[m] * (1 - found)
            pick = jnp.where(take == 1, m, pick)
            row = jnp.where(take == 1, rank[m], row)
            left[m] = left[m] - take
            found = found + take
        spare = spare + 1 - found
        out_ref[PICK + j] = pick
        out_ref[ROW + j] = row
        out_ref[LIVE + j] = found


def routing_table(owner, dirty, slot, local_count):
    return pl.pallas_call(
        functools.partial(table_kernel, local_count),
        out_shape=jax.ShapeDtypeStruct((24,), jnp.int32),
        in_specs=[SMEM] * 3,
        out_specs=SMEM,
        compiler_params=pltpu.CompilerParams(vmem_limit_bytes=VMEM_LIMIT),
        name="routing_table",
    )(owner, dirty, slot)


def pack_kernel(j, count, table_ref, *refs):
    out_ref, sem = refs[-2:]
    for m in range(count):

        @pl.when(table_ref[PICK + j] == m)
        def _():
            pltpu.make_async_copy(refs[m], out_ref, sem).start()

    pltpu.make_async_copy(out_ref, out_ref, sem).wait()


def pack(table, arrived, j, tokens):
    return pl.pallas_call(
        functools.partial(pack_kernel, j, len(arrived)),
        out_shape=jax.ShapeDtypeStruct(arrived[0].shape, arrived[0].dtype),
        in_specs=[SMEM] + [ANY] * (len(arrived) + len(tokens)),
        out_specs=VMEM,
        scratch_shapes=[pltpu.SemaphoreType.DMA],
        compiler_params=pltpu.CompilerParams(vmem_limit_bytes=VMEM_LIMIT),
        name="pack",
    )(table, *arrived, *tokens)


def place_kernel(spots, fresh, table_ref, *refs):
    arrays, refs = refs[: len(spots)], refs[len(spots) :]
    if not fresh:
        acc_in, refs = refs[1], refs[2:]
    out_ref, acc_out, acc_ref, held, sems = refs
    rows, cols = arrays[0].shape
    here = lax.axis_index("rep")
    line = lax.broadcasted_iota(jnp.int32, acc_ref.shape, 0)
    lane = lax.broadcasted_iota(jnp.int32, acc_ref.shape, 1)
    acc_ref[...] = jnp.zeros_like(acc_ref) if fresh else acc_in[...]
    copies = []
    for i, (j, flip) in enumerate(spots):
        first = pl.multiple_of((here ^ flip) * cols, B)
        first_block = (here ^ flip) * (cols // B)
        row = table_ref[ROW + j]
        live = table_ref[LIVE + j] == 1
        at = i * cols

        @pl.when(live)
        def _():
            acc = acc_ref[...]
            for c in range(0, cols, B):
                x = arrays[i][:, c : c + B]
                most = jnp.max(jnp.abs(x), axis=0, keepdims=True).astype(jnp.float32)
                most = jnp.max(most, axis=1, keepdims=True)
                scale = (most + 1e-06).astype(jnp.bfloat16).astype(jnp.float32)
                scaled = x.astype(jnp.float32) * (1.0 / scale)
                held[:, at + c : at + c + B] = scaled.astype(jnp.bfloat16)
                acc = jnp.where((line == row) & (lane == first_block + c // B), scale, acc)
            acc_ref[...] = acc

        @pl.when(jnp.logical_not(live))
        def _():
            held[:, at : at + cols] = jnp.zeros((rows, cols), jnp.bfloat16)

        copies.append(
            pltpu.make_async_copy(
                held.at[:, pl.ds(at, cols)], out_ref.at[row, :, pl.ds(first, cols)], sems.at[i]
            )
        )
        copies[-1].start()

    acc = acc_ref[...]
    acc_out[...] = acc[: acc_out.shape[0], : acc_out.shape[1]].astype(acc_out.dtype)
    for copy in copies:
        copy.wait()


def place(state, table, arrays, spots, replicas, final):
    rows, cols = arrays[0].shape
    fresh = state is None
    kept = jax.ShapeDtypeStruct((8, 128), jnp.float32)
    scales = jax.ShapeDtypeStruct((CAP, cols * replicas // B), jnp.bfloat16)
    return pl.pallas_call(
        functools.partial(place_kernel, spots, fresh),
        out_shape=[
            jax.ShapeDtypeStruct((CAP, rows, cols * replicas), jnp.bfloat16),
            scales if final else kept,
        ],
        in_specs=[SMEM] + [VMEM] * len(arrays) + ([] if fresh else [HBM, VMEM]),
        out_specs=[HBM, VMEM],
        scratch_shapes=[
            pltpu.VMEM(kept.shape, kept.dtype),
            pltpu.VMEM((rows, len(arrays) * cols), jnp.bfloat16),
            pltpu.SemaphoreType.DMA((len(arrays),)),
        ],
        input_output_aliases={} if fresh else {1 + len(arrays): 0},
        compiler_params=pltpu.CompilerParams(vmem_limit_bytes=PLACE_LIMIT),
        cost_estimate=pl.CostEstimate(
            flops=0, bytes_accessed=8 * rows * cols * len(arrays), transcendentals=0
        ),
        name="place",
    )(table, *arrays, *(state or ()))


def gate_kernel(x_ref, *refs):
    pass


def gate(x, *tokens):
    return pl.pallas_call(
        gate_kernel,
        out_shape=jax.ShapeDtypeStruct(x.shape, x.dtype),
        in_specs=[ANY] * (1 + len(tokens)),
        out_specs=ANY,
        input_output_aliases={0: 0},
        compiler_params=pltpu.CompilerParams(vmem_limit_bytes=VMEM_LIMIT),
        name="gate",
    )(x, *tokens)


def pairs(count, flip):
    return [(i, i ^ flip) for i in range(count)]


def paired(trainer_weight, dirty, rollout_owner, rollout_slot):
    replicas, owners = lax.axis_size("rep"), lax.axis_size("exp")
    local_count = trainer_weight.shape[0]

    def over_rep(x, flip):
        return lax.ppermute(x, "rep", pairs(replicas, flip))

    picked = (4, 1, 2, 3, 5, 0, 7, 6)
    outgoing = dict(zip(picked, pick(rollout_owner, trainer_weight, picked)))
    table = routing_table(rollout_owner, dirty, rollout_slot, local_count)
    after = {5: 1, 7: 3, 6: 4}
    got, held, state = {}, {}, None

    def arrival(flip):
        if flip not in got:
            x = outgoing[flip]
            if flip in after:
                x = gate(x, got[after[flip]])
            got[flip] = lax.ppermute(x, "exp", pairs(owners, flip)) if flip else x
        return got[flip]

    def shard(j, flip):
        if (j, flip) not in held:
            if flip == 0:
                tokens = [held[j - 1, 0], state[1]] if j == CAP - 1 else []
                held[j, 0] = pack(table, [arrival(f) for f in ORDER[: LIMIT[j]]], j, tokens)
            else:
                held[j, flip] = over_rep(held[j, 2 if flip == 3 else 0], 1 if flip & 1 else 2)
        return held[j, flip]

    for wave in WAVES:
        spots = tuple((j, flip) for j, flips in wave for flip in flips)
        arrays = [shard(j, flip) for j, flip in spots]
        state = place(state, table, arrays, spots, replicas, wave is WAVES[-1])
    tiles, scales = state
    return tiles, scales[:, None, :]


def quantize(weights):
    count, rows, cols = weights.shape
    blocks = weights.astype(jnp.float32).reshape(count, rows // B, B, cols // B, B)
    largest = jnp.max(jnp.abs(blocks), axis=(2, 4))
    scale = (largest + 1e-06).astype(jnp.bfloat16)
    divisor = lax.optimization_barrier(scale).astype(jnp.float32)
    scaled = (blocks / divisor[:, :, None, :, None]).reshape(count, rows, cols).astype(jnp.bfloat16)
    return (scaled, scale)


def gathered(trainer_weight, dirty, rollout_owner, rollout_slot):
    owners = lax.axis_size("exp")
    here = lax.axis_index("exp")
    local_count = trainer_weight.shape[0]
    experts = dirty.shape[0]
    live = dirty == 1
    earlier = (
        (rollout_owner[:, None] == rollout_owner[None, :])
        & live[None, :]
        & (rollout_slot[None, :] < rollout_slot[:, None])
    )
    rank = jnp.sum(earlier.astype(jnp.int32), axis=1)
    start = here * local_count
    local_owner = lax.dynamic_slice_in_dim(rollout_owner, start, local_count)
    local_live = lax.dynamic_slice_in_dim(live, start, local_count)
    peers = jnp.arange(owners, dtype=jnp.int32)
    outgoing = ((local_owner[None, :] == peers[:, None]) & local_live[None, :]).astype(jnp.bfloat16)
    slots = jnp.arange(CAP, dtype=jnp.int32)
    wanted = (
        live[None, :] & (rollout_owner[None, :] == here) & (rank[None, :] == slots[:, None])
    ).astype(jnp.float32)
    source = (
        jnp.arange(experts, dtype=jnp.int32)[:, None] // local_count == peers[None, :]
    ).astype(jnp.float32)
    pick = jnp.dot(
        wanted, source, precision=lax.Precision.HIGHEST, preferred_element_type=jnp.float32
    )
    pick_low = pick.astype(jnp.bfloat16)
    scaled, scale = quantize(trainer_weight)
    send_tiles = jnp.einsum(
        "pj,jsd->psd", outgoing, scaled, preferred_element_type=jnp.float32
    ).astype(jnp.bfloat16)
    send_scales = jnp.einsum(
        "pj,jab->pab", outgoing, scale, preferred_element_type=jnp.float32
    ).astype(jnp.bfloat16)
    got_tiles, got_scales = (
        lax.all_to_all(send_tiles, "exp", split_axis=0, concat_axis=0, tiled=True),
        lax.all_to_all(send_scales, "exp", split_axis=0, concat_axis=0, tiled=True),
    )
    tiles = jnp.einsum(
        "cp,psd->csd", pick_low, got_tiles, preferred_element_type=jnp.float32
    ).astype(jnp.bfloat16)
    scales = jnp.einsum(
        "cp,pab->cab", pick_low, got_scales, preferred_element_type=jnp.float32
    ).astype(jnp.bfloat16)
    update_tiles, update_scales = (
        lax.all_gather(tiles, "rep", axis=2, tiled=True),
        lax.all_gather(scales, "rep", axis=2, tiled=True),
    )
    return (update_tiles, update_scales)


def on_device(trainer_weight, dirty, rollout_owner, rollout_slot):
    local_count, rows, cols = trainer_weight.shape
    replicas, owners = lax.axis_size("rep"), lax.axis_size("exp")
    if (replicas, owners, local_count, rows) == (4, len(ORDER), len(ORDER), B) and cols % B == 0:
        return paired(trainer_weight, dirty, rollout_owner, rollout_slot)
    return gathered(trainer_weight, dirty, rollout_owner, rollout_slot)


def solution(mesh):
    in_specs = (P("exp", None, "rep"), P(), P(), P())
    out_specs = (P("exp", None, None), P("exp", None, None))
    return jax.shard_map(
        on_device, mesh=mesh, in_specs=in_specs, out_specs=out_specs, check_vma=False
    )
```
